32 devices in a mesh: row: 4 (over x, core), col: 8 (over z, y).
Axes of the slice: x: 2, y: 2, z: 4, core: 2. Of those that a mesh axis runs over, the one named last changes fastest.
Arguments:
- vectors: float32 [8192, 512], P(('row', 'col')), may hold values from -6 to 6
- hamiltonian_blocks: float32 [192, 128, 128], P(('row', 'col')), may hold values from -0.3125 to 0.3125
- block_place: int32 [192, 3], P(('row', 'col')), may hold values from 0 to 2, as said below
- live_count: int32 [32], P(('row', 'col')), may hold values from 1 to 6, as said below
- spectrum: float32 [2], replicated, may hold values from 1.5 to 3
Outputs:
- filtered: float32 [8192, 512], P(('row', 'col'))
The draws below stay inside these ranges and needn't reach their ends.
Inputs may be any that keep to these rules, and one draw needn't show every extreme that they name: `block_place`: each row holds a block row within a domain, a domain code from 0 to 2, and a block column within a domain. `live_count`: some domain uses all 6 slots.
All inputs are finite; a program needn't handle non-finite values.
Results may differ from the reference program's by a relative error of at most 0.0001.
Values sent between devices are 32-bit elements; how exact they have to be, the bound alone decides.
A program may use at most 64 MiB of HBM per device.

```python
import jax
import jax.numpy as jnp
from jax import lax

BS = 128
M = 512
BR = 2
SLOTS = 6
NDEV = 32
ORDER = 8192
N_ROW = 4
N_COL = 8


def draw_block_place(key, part):
    keys = jax.random.split(jax.random.fold_in(key, 11), 3)
    count = NDEV * SLOTS
    row_pick = jax.random.randint(keys[0], (count,), 0, BR)
    domain_pick = jax.random.randint(keys[1], (count,), 0, 3)
    col_pick = jax.random.randint(keys[2], (count,), 0, BR)
    return jnp.stack([row_pick, domain_pick, col_pick], axis=1).astype(jnp.int32)


def draw_live_count(key, part):
    keys = jax.random.split(jax.random.fold_in(key, 23), 2)
    counts = jax.random.randint(keys[0], (NDEV,), 1, SLOTS + 1)
    fullest = jax.random.randint(keys[1], (), 0, NDEV)
    return counts.at[fullest].set(SLOTS).astype(jnp.int32)


def levels(own_key, shape, cuts, smallest, high):
    def one(position, shards_of):
        heights = jax.random.uniform(jax.random.fold_in(jax.random.fold_in(own_key, 6), position), (shards_of,), jnp.float32, smallest / len(cuts), high / len(cuts))
        return jnp.repeat(jnp.exp(heights), shape[position] // shards_of).reshape((-1,) + (1,) * (len(shape) - position - 1))

    level = one(*cuts[0])
    for cut in cuts[1:]:
        level = level * one(*cut)
    return level


def bell_draw(stream_key, dims, spread, limit, pieces=(), dtype=jnp.bfloat16):
    drawn = spread * jax.random.normal(stream_key, dims, jnp.float32)
    if pieces:
        drawn = drawn * levels(stream_key, dims, pieces, -0.22, 0.18)
    return jnp.clip(drawn, -limit, limit).astype(dtype)


def setup_inputs(seed: int = 0) -> dict:
    seeds = jax.random.split(jax.random.key(seed), 6)
    return {
        "vectors": bell_draw(seeds[0], (ORDER, M), 1.0, 6.0, ((0, 32),), jnp.float32),
        "hamiltonian_blocks": bell_draw(seeds[1], (NDEV * SLOTS, BS, BS), (BS * SLOTS // 2) ** -0.5, 0.3125, ((0, 32),), jnp.float32),
        "block_place": draw_block_place(jax.random.fold_in(seeds[5], 71), 0),
        "live_count": draw_live_count(jax.random.fold_in(seeds[5], 71), 0),
        "spectrum": jnp.clip(jax.random.uniform(seeds[4], (2,), jnp.float32, 1.5, 3.0), 1.5, 3.0),
    }


def apply_hamiltonian(field, hamiltonian_blocks, block_place, live_count):
    def add_slot(flat_index, total):
        device = flat_index // SLOTS
        slot_index = flat_index % SLOTS
        grid_row = device // N_COL
        grid_col = device % N_COL
        targets = block_place[flat_index, 1]
        east_domain = grid_row * N_COL + (grid_col + 1) % N_COL
        south_domain = ((grid_row + 1) % N_ROW) * N_COL + grid_col
        neighbour = jnp.where(targets == 0, device, jnp.where(targets == 1, east_domain, south_domain))
        first_row = ((device * BR + block_place[flat_index, 0]) * BS).astype(jnp.int32)
        second_row = ((neighbour * BR + block_place[flat_index, 2]) * BS).astype(jnp.int32)
        weight = jnp.where(slot_index < live_count[device], 1.0, 0.0).astype(jnp.float32)
        block = hamiltonian_blocks[flat_index] * weight
        left_panel = lax.dynamic_slice_in_dim(field, first_row, BS, 0)
        right_panel = lax.dynamic_slice_in_dim(field, second_row, BS, 0)
        forward = jnp.dot(block, right_panel, preferred_element_type=jnp.float32, precision=lax.Precision.HIGHEST)
        current = lax.dynamic_slice_in_dim(total, first_row, BS, 0)
        total = lax.dynamic_update_slice_in_dim(total, current + forward, first_row, 0)
        backward = jnp.dot(block.T, left_panel, preferred_element_type=jnp.float32, precision=lax.Precision.HIGHEST)
        current = lax.dynamic_slice_in_dim(total, second_row, BS, 0)
        total = lax.dynamic_update_slice_in_dim(total, current + backward, second_row, 0)
        return total

    return lax.fori_loop(0, NDEV * SLOTS, add_slot, jnp.zeros_like(field))


def reference(vectors, hamiltonian_blocks, block_place, live_count, spectrum):
    centre = spectrum[0]
    half_width = spectrum[1]
    image = apply_hamiltonian(vectors, hamiltonian_blocks, block_place, live_count)
    first = (image - centre * vectors) / half_width
    image = apply_hamiltonian(first, hamiltonian_blocks, block_place, live_count)
    return 2.0 * (image - centre * first) / half_width - vectors
```

```python
import functools

import jax
import jax.numpy as jnp
from jax import lax
from jax.experimental import pallas as pl
from jax.experimental.pallas import tpu as pltpu
from jax.sharding import PartitionSpec as P


CHUNKS = 2
SYM, FWD_EAST, BACK_EAST, FWD_SOUTH, BACK_SOUTH = range(5)
MESH = pl.DeviceIdType.MESH


def split_rows(x):
    high = x.astype(jnp.bfloat16)
    low = (x - high.astype(jnp.float32)).astype(jnp.bfloat16)
    return jnp.concatenate([high, high, low], axis=0)


def split_columns(x):
    high = x.astype(jnp.bfloat16)
    low = (x - high.astype(jnp.float32)).astype(jnp.bfloat16)
    return jnp.concatenate([high, low, high], axis=1)


def product(matrix, x):
    return jnp.dot(matrix, x, preferred_element_type=jnp.float32)


def kernel(
    row_count,
    col_count,
    vec_ref,
    blocks_ref,
    place_ref,
    live_ref,
    spectrum_ref,
    out_ref,
    code,
    code_in,
    blocks_in,
    dense,
    mats,
    field,
    south,
    south_out,
    north_in,
    east,
    east_out,
    west_in,
    acc,
    send_sem,
    recv_sem,
):
    rows, width = vec_ref.shape
    slots, bs, _ = blocks_ref.shape
    panels = rows // bs
    half = width // 2
    wide = half // CHUNKS

    me_row, me_col = lax.axis_index("row"), lax.axis_index("col")
    mine = lax.rem(me_col, 2)
    other = 1 - mine
    to_partner = (me_row, me_col + 1 - 2 * mine)
    to_north = (lax.rem(me_row + row_count - 1, row_count), me_col)
    to_south = (lax.rem(me_row + 1, row_count), me_col)
    to_west = (me_row, lax.rem(me_col + col_count - 2, col_count))
    to_east = (me_row, lax.rem(me_col + 2, col_count))

    barrier = pltpu.get_barrier_semaphore()
    for device in (to_partner, to_north, to_south, to_west, to_east):
        pl.semaphore_signal(barrier, inc=1, device_id=device, device_id_type=MESH)

    live = live_ref[0]
    for s in range(slots):
        value = (place_ref[s, 0] * 3 + place_ref[s, 1]) * panels + place_ref[s, 2]
        value = jnp.where(s < live, value, -1)
        code[s : s + 1, :] = jnp.full((1, bs), value, jnp.int32).astype(jnp.float32)
    pl.semaphore_wait(barrier, 5)

    started = []

    def send(src, dst, device):
        index = len(started)
        copy = pltpu.make_async_remote_copy(
            src_ref=src,
            dst_ref=dst,
            send_sem=send_sem.at[index],
            recv_sem=recv_sem.at[index],
            device_id=device,
            device_id_type=MESH,
        )
        copy.start()
        started.append(copy)
        return copy

    def columns(which, q):
        return pl.ds(pl.multiple_of(which * half + q * wide, wide), wide)

    got_code = send(code, code_in, to_partner)
    got_blocks = send(blocks_ref, blocks_in, to_partner)
    got_field = [
        send(vec_ref.at[:, columns(other, q)], field.at[0, q, mine], to_partner) for q in range(CHUNKS)
    ]
    arrivals = [[[] for _ in range(CHUNKS)] for _ in range(2)]
    for q in range(CHUNKS):
        arrivals[0][q].append(send(vec_ref.at[:, columns(mine, q)], south.at[0, q, mine], to_north))

    def assemble(source, codes, domain):
        for t in range(3):
            for a in range(panels):
                for b in range(panels):
                    total = None
                    for s in range(slots):
                        weight = jnp.where(codes[s : s + 1, :] == float((a * 3 + t) * panels + b), 1.0, 0.0)
                        term = source[s] * weight
                        total = term if total is None else total + term
                    dense[t, a * bs : (a + 1) * bs, b * bs : (b + 1) * bs] = total
        own = dense[0]
        mats[domain, SYM] = split_columns(own + own.T)
        for t, forward, back in ((1, FWD_EAST, BACK_EAST), (2, FWD_SOUTH, BACK_SOUTH)):
            matrix = dense[t]
            mats[domain, forward] = split_columns(matrix)
            mats[domain, back] = split_columns(matrix.T)

    assemble(blocks_ref, code, mine)
    for q in range(CHUNKS):
        x = vec_ref[:, columns(mine, q)]
        field[0, q, mine] = x
        south_out[0, q, mine] = product(mats[mine, BACK_SOUTH], split_rows(x))
        arrivals[0][q].append(send(south_out.at[0, q, mine], north_in.at[0, q, mine], to_south))

    got_code.wait_recv()
    got_blocks.wait_recv()
    assemble(blocks_in, code_in, other)

    def inside(step, q):
        first, second = split_rows(field[step, q, 0]), split_rows(field[step, q, 1])
        east_out[step, q] = product(mats[1, BACK_EAST], second)
        arrivals[step][q].append(send(east_out.at[step, q], west_in.at[step, q], to_east))
        if step == 1:
            south_out[step, q, 0] = product(mats[0, BACK_SOUTH], first)
            south_out[step, q, 1] = product(mats[1, BACK_SOUTH], second)
            arrivals[step][q].append(send(south_out.at[step, q], north_in.at[step, q], to_south))
        acc[q, 0] = product(mats[0, SYM], first) + product(mats[0, FWD_EAST], second)
        acc[q, 1] = product(mats[0, BACK_EAST], first) + product(mats[1, SYM], second)

    for q in range(CHUNKS):
        got_field[q].wait_recv()
        arrivals[0][q].append(send(field.at[0, q, other], south.at[0, q, other], to_north))
        arrivals[0][q].append(send(field.at[0, q, 0], east.at[0, q], to_west))
        south_out[0, q, other] = product(mats[other, BACK_SOUTH], split_rows(field[0, q, other]))
        arrivals[0][q].append(send(south_out.at[0, q, other], north_in.at[0, q, other], to_south))
        inside(0, q)

    centre = spectrum_ref[0]
    inverse = 1.0 / spectrum_ref[1]

    def finish(step, q):
        for copy in arrivals[step][q]:
            copy.wait_recv()
        upper = acc[q, 0] + product(mats[0, FWD_SOUTH], split_rows(south[step, q, 0]))
        upper = upper + north_in[step, q, 0] + west_in[step, q]
        lower = acc[q, 1] + product(mats[1, FWD_SOUTH], split_rows(south[step, q, 1]))
        lower = lower + product(mats[1, FWD_EAST], split_rows(east[step, q])) + north_in[step, q, 1]
        return (
            (upper - centre * field[step, q, 0]) * inverse,
            (lower - centre * field[step, q, 1]) * inverse,
        )

    for q in range(CHUNKS):
        upper, lower = finish(0, q)
        field[1, q, 0] = upper
        field[1, q, 1] = lower
        arrivals[1][q].append(send(field.at[1, q], south.at[1, q], to_north))
        arrivals[1][q].append(send(field.at[1, q, 0], east.at[1, q], to_west))
        inside(1, q)

    last = []
    for q in range(CHUNKS):
        upper, lower = finish(1, q)
        field[2, q, 0] = 2.0 * upper - field[0, q, 0]
        field[2, q, 1] = 2.0 * lower - field[0, q, 1]
        last.append(send(field.at[2, q, other], out_ref.at[:, columns(mine, q)], to_partner))
        out_ref[:, columns(mine, q)] = field[2, q, mine]

    for copy in last:
        copy.wait_recv()
    for copy in started:
        copy.wait_send()


def local(row_count, col_count, vectors, blocks, place, live, spectrum):
    rows, width = vectors.shape
    slots, bs, _ = blocks.shape
    wide = width // 2 // CHUNKS
    f32 = jnp.float32
    copies = 4 + CHUNKS * (1 + 1 + 2 + 1 + 1 + 2 + 2 + 1)
    vmem = pl.BlockSpec(memory_space=pltpu.VMEM)
    smem = pl.BlockSpec(memory_space=pltpu.SMEM)
    return pl.pallas_call(
        functools.partial(kernel, row_count, col_count),
        out_shape=jax.ShapeDtypeStruct((rows, width), f32),
        in_specs=[vmem, vmem, smem, smem, smem],
        out_specs=vmem,
        scratch_shapes=[
            pltpu.VMEM((8, bs), f32),
            pltpu.VMEM((8, bs), f32),
            pltpu.VMEM((slots, bs, bs), f32),
            pltpu.VMEM((3, rows, rows), f32),
            pltpu.VMEM((2, 5, rows, 3 * rows), jnp.bfloat16),
            pltpu.VMEM((3, CHUNKS, 2, rows, wide), f32),
            pltpu.VMEM((2, CHUNKS, 2, rows, wide), f32),
            pltpu.VMEM((2, CHUNKS, 2, rows, wide), f32),
            pltpu.VMEM((2, CHUNKS, 2, rows, wide), f32),
            pltpu.VMEM((2, CHUNKS, rows, wide), f32),
            pltpu.VMEM((2, CHUNKS, rows, wide), f32),
            pltpu.VMEM((2, CHUNKS, rows, wide), f32),
            pltpu.VMEM((CHUNKS, 2, rows, wide), f32),
            pltpu.SemaphoreType.DMA((copies,)),
            pltpu.SemaphoreType.DMA((copies,)),
        ],
        compiler_params=pltpu.CompilerParams(
            collective_id=0, has_side_effects=True, vmem_limit_bytes=32 * 1024 * 1024
        ),
        name="chebyshev_pair",
    )(vectors, blocks, place, live, spectrum)


def solution(mesh):
    return jax.shard_map(
        functools.partial(local, mesh.shape["row"], mesh.shape["col"]),
        mesh=mesh,
        in_specs=(
            P(("row", "col"), None),
            P(("row", "col"), None, None),
            P(("row", "col"), None),
            P(("row", "col")),
            P(),
        ),
        out_specs=P(("row", "col"), None),
        check_vma=False,
    )
```

```python
import functools

import jax
import jax.numpy as jnp
from jax import lax
from jax.experimental import pallas as pl
from jax.experimental.pallas import tpu as pltpu
from jax.sharding import PartitionSpec as P


CHUNKS = 2
SYM, FWD_EAST, BACK_EAST, FWD_SOUTH, BACK_SOUTH = range(5)
MESH = pl.DeviceIdType.MESH


def split_rows(x):
    high = x.astype(jnp.bfloat16)
    low = (x - high.astype(jnp.float32)).astype(jnp.bfloat16)
    return jnp.concatenate([high, high, low], axis=0)


def split_columns(x):
    high = x.astype(jnp.bfloat16)
    low = (x - high.astype(jnp.float32)).astype(jnp.bfloat16)
    return jnp.concatenate([high, low, high], axis=1)


def product(matrix, x):
    return jnp.dot(matrix, x, preferred_element_type=jnp.float32)


def kernel(
    row_count,
    col_count,
    vec_hbm,
    blocks_hbm,
    place_ref,
    live_ref,
    spectrum_ref,
    out_ref,
    vec_ref,
    blocks_ref,
    code,
    code_in,
    blocks_in,
    mats,
    field,
    south,
    south_out,
    north_in,
    east,
    east_out,
    west_in,
    acc,
    load_sem,
    send_sem,
    recv_sem,
):
    rows, width = vec_ref.shape
    slots, bs, _ = blocks_ref.shape
    panels = rows // bs
    half = width // 2
    wide = half // CHUNKS

    load_blocks = pltpu.make_async_copy(blocks_hbm, blocks_ref, load_sem.at[0])
    load_blocks.start()
    load_vec = pltpu.make_async_copy(vec_hbm, vec_ref, load_sem.at[1])
    load_vec.start()

    me_row, me_col = lax.axis_index("row"), lax.axis_index("col")
    mine = lax.rem(me_col, 2)
    other = 1 - mine
    to_partner = (me_row, me_col + 1 - 2 * mine)
    to_north = (lax.rem(me_row + row_count - 1, row_count), me_col)
    to_south = (lax.rem(me_row + 1, row_count), me_col)
    to_west = (me_row, lax.rem(me_col + col_count - 2, col_count))
    to_east = (me_row, lax.rem(me_col + 2, col_count))

    barrier = pltpu.get_barrier_semaphore()
    for device in (to_partner, to_north, to_south, to_west, to_east):
        pl.semaphore_signal(barrier, inc=1, device_id=device, device_id_type=MESH)

    live = live_ref[0]
    for s in range(slots):
        value = (place_ref[0, s] * 3 + place_ref[1, s]) * panels + place_ref[2, s]
        value = jnp.where(s < live, value, -1)
        code[s : s + 1, :] = jnp.full((1, bs), value, jnp.int32).astype(jnp.float32)
    pl.semaphore_wait(barrier, 5)

    made = []

    def remote(src, dst, device, reuse=None):
        index = len(made) if reuse is None else reuse
        copy = pltpu.make_async_remote_copy(
            src_ref=src,
            dst_ref=dst,
            send_sem=send_sem.at[index],
            recv_sem=recv_sem.at[index],
            device_id=device,
            device_id_type=MESH,
        )
        if reuse is None:
            made.append(copy)
        return copy

    def send(src, dst, device):
        copy = remote(src, dst, device)
        copy.start()
        return copy

    def columns(which, q):
        return pl.ds(pl.multiple_of(which * half + q * wide, wide), wide)

    def even(body):
        pl.when(mine == 0)(body)

    def odd(body):
        pl.when(mine == 1)(body)

    chunks = range(CHUNKS)
    both = range(2)

    got_field = [send(vec_hbm.at[:, columns(other, 0)], field.at[0, 0, mine], to_partner)]
    got_code = send(code, code_in, to_partner)
    got_blocks = send(blocks_hbm, blocks_in, to_partner)
    for q in chunks[1:]:
        got_field.append(send(vec_hbm.at[:, columns(other, q)], field.at[0, q, mine], to_partner))

    south_copy = [[[None] * 2 for _ in chunks] for _ in both]
    north_copy = [[[None] * 2 for _ in chunks] for _ in both]
    for step in both:
        for q in chunks:
            for i, d in enumerate((mine, other)):
                src = field.at[step, q, d]
                if step == 0 and i == 0:
                    src = vec_hbm.at[:, columns(mine, q)]
                south_copy[step][q][i] = remote(src, south.at[step, q, d], to_north)
                north_copy[step][q][i] = remote(south_out.at[step, q, d], north_in.at[step, q, d], to_south)
    east_index = len(made)
    east_copy = [[remote(field.at[step, q, 0], east.at[step, q], to_west) for q in chunks] for step in both]
    west_copy = [[remote(east_out.at[step, q], west_in.at[step, q], to_east) for q in chunks] for step in both]
    early = [
        remote(vec_hbm.at[:, columns(mine, q)], east.at[0, q], to_west, east_index + q) for q in chunks
    ]

    for q in chunks:
        even(early[q].start)
        south_copy[0][q][0].start()

    def dense(source, codes, t):
        columns_of = []
        for b in range(panels):
            parts = []
            for a in range(panels):
                total = None
                for s in range(slots):
                    weight = jnp.where(codes[s : s + 1, :] == float((a * 3 + t) * panels + b), 1.0, 0.0)
                    term = source[s] * weight
                    total = term if total is None else total + term
                parts.append(total)
            columns_of.append(jnp.concatenate(parts, axis=0))
        return jnp.concatenate(columns_of, axis=1)

    def assemble_side(source, codes, domain, t, forward, back):
        matrix = dense(source, codes, t)
        mats[domain, back] = split_columns(matrix.T)
        mats[domain, forward] = split_columns(matrix)

    def assemble_own(source, codes, domain):
        matrix = dense(source, codes, 0)
        mats[domain, SYM] = split_columns(matrix + matrix.T)

    def push_east(step, q):
        east_out[step, q] = product(mats[1, BACK_EAST], split_rows(field[step, q, 1]))
        west_copy[step][q].start()

    def push_south(step, q, i, d):
        south_out[step, q, d] = product(mats[d, BACK_SOUTH], split_rows(field[step, q, d]))
        north_copy[step][q][i].start()

    load_vec.wait()
    for q in chunks:
        field[0, q, mine] = vec_ref[:, columns(mine, q)]
    load_blocks.wait()
    assemble_side(blocks_ref, code, mine, 1, FWD_EAST, BACK_EAST)

    @odd
    def _():
        for q in chunks:
            push_east(0, q)

    assemble_side(blocks_ref, code, mine, 2, FWD_SOUTH, BACK_SOUTH)
    for q in chunks:
        push_south(0, q, 0, mine)
    assemble_own(blocks_ref, code, mine)

    got_field[0].wait_recv()
    odd(east_copy[0][0].start)
    south_copy[0][0][1].start()

    got_code.wait_recv()
    got_blocks.wait_recv()
    assemble_side(blocks_in, code_in, other, 1, FWD_EAST, BACK_EAST)

    @even
    def _():
        push_east(0, 0)

    assemble_side(blocks_in, code_in, other, 2, FWD_SOUTH, BACK_SOUTH)
    push_south(0, 0, 1, other)
    for q in chunks[1:]:
        got_field[q].wait_recv()
        odd(east_copy[0][q].start)
        south_copy[0][q][1].start()

        @even
        def _():
            push_east(0, q)

        push_south(0, q, 1, other)
    assemble_own(blocks_in, code_in, other)

    def inside(step, q):
        first, second = split_rows(field[step, q, 0]), split_rows(field[step, q, 1])
        acc[q, 0] = product(mats[0, SYM], first) + product(mats[0, FWD_EAST], second)
        acc[q, 1] = product(mats[0, BACK_EAST], first) + product(mats[1, SYM], second)

    for q in chunks:
        inside(0, q)

    centre = spectrum_ref[0]
    inverse = 1.0 / spectrum_ref[1]

    def wait_row(step, q, i):
        south_copy[step][q][i].wait_recv()
        north_copy[step][q][i].wait_recv()

    def upper(step, q):
        total = acc[q, 0] + product(mats[0, FWD_SOUTH], split_rows(south[step, q, 0]))
        total = total + north_in[step, q, 0]
        west_copy[step][q].wait_recv()
        return (total + west_in[step, q] - centre * field[step, q, 0]) * inverse

    def lower(step, q):
        total = acc[q, 1] + product(mats[1, FWD_SOUTH], split_rows(south[step, q, 1]))
        total = total + north_in[step, q, 1]
        east_copy[step][q].wait_recv()
        total = total + product(mats[1, FWD_EAST], split_rows(east[step, q]))
        return (total - centre * field[step, q, 1]) * inverse

    for q in chunks:
        wait_row(0, q, 0)
        wait_row(0, q, 1)
        field[1, q, 0] = upper(0, q)
        even(east_copy[1][q].start)
        field[1, q, 1] = lower(0, q)
        south_copy[1][q][1].start()
        push_east(1, q)
        odd(east_copy[1][q].start)
        push_south(1, q, 1, other)
        south_copy[1][q][0].start()
        push_south(1, q, 0, mine)
        inside(1, q)

    last = [remote(field.at[2, q, other], out_ref.at[:, columns(mine, q)], to_partner) for q in chunks]

    def set_upper(q):
        field[2, q, 0] = 2.0 * upper(1, q) - field[0, q, 0]

    def set_lower(q):
        field[2, q, 1] = 2.0 * lower(1, q) - field[0, q, 1]

    for q in chunks:
        wait_row(1, q, 1)
        even(functools.partial(set_lower, q))
        odd(functools.partial(set_upper, q))
        last[q].start()
        wait_row(1, q, 0)
        even(functools.partial(set_upper, q))
        odd(functools.partial(set_lower, q))
        out_ref[:, columns(mine, q)] = field[2, q, mine]

    for copy in last:
        copy.wait_recv()
    for copy in made:
        copy.wait_send()


def local(row_count, col_count, vectors, blocks, place, live, spectrum):
    rows, width = vectors.shape
    slots, bs, _ = blocks.shape
    wide = width // 2 // CHUNKS
    f32 = jnp.float32
    copies = 2 + CHUNKS * (1 + 4 + 4 + 2 + 2 + 1)
    vmem = pl.BlockSpec(memory_space=pltpu.VMEM)
    hbm = pl.BlockSpec(memory_space=pltpu.HBM)
    smem = pl.BlockSpec(memory_space=pltpu.SMEM)
    return pl.pallas_call(
        functools.partial(kernel, row_count, col_count),
        out_shape=jax.ShapeDtypeStruct((rows, width), f32),
        in_specs=[hbm, hbm, smem, smem, smem],
        out_specs=vmem,
        scratch_shapes=[
            pltpu.VMEM((rows, width), f32),
            pltpu.VMEM((slots, bs, bs), f32),
            pltpu.VMEM((8, bs), f32),
            pltpu.VMEM((8, bs), f32),
            pltpu.VMEM((slots, bs, bs), f32),
            pltpu.VMEM((2, 5, rows, 3 * rows), jnp.bfloat16),
            pltpu.VMEM((3, CHUNKS, 2, rows, wide), f32),
            pltpu.VMEM((2, CHUNKS, 2, rows, wide), f32),
            pltpu.VMEM((2, CHUNKS, 2, rows, wide), f32),
            pltpu.VMEM((2, CHUNKS, 2, rows, wide), f32),
            pltpu.VMEM((2, CHUNKS, rows, wide), f32),
            pltpu.VMEM((2, CHUNKS, rows, wide), f32),
            pltpu.VMEM((2, CHUNKS, rows, wide), f32),
            pltpu.VMEM((CHUNKS, 2, rows, wide), f32),
            pltpu.SemaphoreType.DMA((2,)),
            pltpu.SemaphoreType.DMA((copies,)),
            pltpu.SemaphoreType.DMA((copies,)),
        ],
        compiler_params=pltpu.CompilerParams(
            collective_id=0, has_side_effects=True, vmem_limit_bytes=60 * 1024 * 1024
        ),
        name="chebyshev_pair",
    )(vectors, blocks, place.T, live, spectrum)


def solution(mesh):
    return jax.shard_map(
        functools.partial(local, mesh.shape["row"], mesh.shape["col"]),
        mesh=mesh,
        in_specs=(
            P(("row", "col"), None),
            P(("row", "col"), None, None),
            P(("row", "col"), None),
            P(("row", "col")),
            P(),
        ),
        out_specs=P(("row", "col"), None),
        check_vma=False,
    )
```

```python
import functools

import jax
import jax.numpy as jnp
from jax import lax
from jax.experimental import pallas as pl
from jax.experimental.pallas import tpu as pltpu
from jax.sharding import PartitionSpec as P


CHUNKS = 2
SYM, FWD_EAST, BACK_EAST, FWD_SOUTH, BACK_SOUTH = range(5)
MESH = pl.DeviceIdType.MESH


def split_rows(x):
    high = x.astype(jnp.bfloat16)
    low = (x - high.astype(jnp.float32)).astype(jnp.bfloat16)
    return jnp.concatenate([high, high, low], axis=0)


def split_columns(x):
    high = x.astype(jnp.bfloat16)
    low = (x - high.astype(jnp.float32)).astype(jnp.bfloat16)
    return jnp.concatenate([high, low, high], axis=1)


def product(matrix, x):
    return jnp.dot(matrix, x, preferred_element_type=jnp.float32)


def kernel(
    row_count,
    col_count,
    vec_hbm,
    blocks_hbm,
    place_ref,
    live_ref,
    spectrum_ref,
    out_ref,
    vec_ref,
    blocks_ref,
    code,
    code_in,
    blocks_in,
    mats,
    field,
    south,
    south_out,
    north_in,
    east,
    east_out,
    west_in,
    acc,
    load_sem,
    send_sem,
    recv_sem,
):
    rows, width = vec_ref.shape
    slots, bs, _ = blocks_ref.shape
    panels = rows // bs
    half = width // 2
    wide = half // CHUNKS

    load_blocks = pltpu.make_async_copy(blocks_hbm, blocks_ref, load_sem.at[0])
    load_blocks.start()
    load_vec = pltpu.make_async_copy(vec_hbm, vec_ref, load_sem.at[1])
    load_vec.start()

    me_row, me_col = lax.axis_index("row"), lax.axis_index("col")
    mine = lax.rem(me_col, 2)
    other = 1 - mine
    to_partner = (me_row, me_col + 1 - 2 * mine)
    to_north = (lax.rem(me_row + row_count - 1, row_count), me_col)
    to_south = (lax.rem(me_row + 1, row_count), me_col)
    to_west = (me_row, lax.rem(me_col + col_count - 2, col_count))
    to_east = (me_row, lax.rem(me_col + 2, col_count))

    barrier = pltpu.get_barrier_semaphore()
    for device in (to_partner, to_north, to_south, to_west, to_east):
        pl.semaphore_signal(barrier, inc=1, device_id=device, device_id_type=MESH)

    live = live_ref[0]
    for s in range(slots):
        value = (place_ref[0, s] * 3 + place_ref[1, s]) * panels + place_ref[2, s]
        value = jnp.where(s < live, value, -1)
        code[s : s + 1, :] = jnp.full((1, bs), value, jnp.int32).astype(jnp.float32)
    pl.semaphore_wait(barrier, 5)

    made = []

    def remote(src, dst, device, reuse=None):
        index = len(made) if reuse is None else reuse
        copy = pltpu.make_async_remote_copy(
            src_ref=src,
            dst_ref=dst,
            send_sem=send_sem.at[index],
            recv_sem=recv_sem.at[index],
            device_id=device,
            device_id_type=MESH,
        )
        if reuse is None:
            made.append(copy)
        return copy

    def send(src, dst, device):
        copy = remote(src, dst, device)
        copy.start()
        return copy

    def columns(which, q):
        return pl.ds(pl.multiple_of(which * half + q * wide, wide), wide)

    def even(body):
        pl.when(mine == 0)(body)

    def odd(body):
        pl.when(mine == 1)(body)

    chunks = range(CHUNKS)
    both = range(2)

    got_field = [send(vec_hbm.at[:, columns(other, 0)], field.at[0, 0, mine], to_partner)]
    got_code = send(code, code_in, to_partner)
    got_blocks = send(blocks_hbm, blocks_in, to_partner)
    for q in chunks[1:]:
        got_field.append(send(vec_hbm.at[:, columns(other, q)], field.at[0, q, mine], to_partner))

    south_copy = [[[None] * 2 for _ in chunks] for _ in both]
    north_copy = [[[None] * 2 for _ in chunks] for _ in both]
    for step in both:
        for q in chunks:
            for i, d in enumerate((mine, other)):
                src = field.at[step, q, d]
                if step == 0 and i == 0:
                    src = vec_hbm.at[:, columns(mine, q)]
                south_copy[step][q][i] = remote(src, south.at[step, q, d], to_north)
                north_copy[step][q][i] = remote(south_out.at[step, q, d], north_in.at[step, q, d], to_south)
    east_index = len(made)
    east_copy = [[remote(field.at[step, q, 0], east.at[step, q], to_west) for q in chunks] for step in both]
    west_copy = [[remote(east_out.at[step, q], west_in.at[step, q], to_east) for q in chunks] for step in both]
    early = [
        remote(vec_hbm.at[:, columns(mine, q)], east.at[0, q], to_west, east_index + q) for q in chunks
    ]

    for q in chunks:
        even(early[q].start)
        south_copy[0][q][0].start()

    def dense(source, codes, t):
        columns_of = []
        for b in range(panels):
            parts = []
            for a in range(panels):
                total = None
                for s in range(slots):
                    weight = jnp.where(codes[s : s + 1, :] == float((a * 3 + t) * panels + b), 1.0, 0.0)
                    term = source[s] * weight
                    total = term if total is None else total + term
                parts.append(total)
            columns_of.append(jnp.concatenate(parts, axis=0))
        return jnp.concatenate(columns_of, axis=1)

    def assemble_side(source, codes, domain, t, forward, back):
        matrix = dense(source, codes, t)
        mats[domain, back] = split_columns(matrix.T)
        mats[domain, forward] = split_columns(matrix)

    def assemble_own(source, codes, domain):
        matrix = dense(source, codes, 0)
        mats[domain, SYM] = split_columns(matrix + matrix.T)

    def push_east(step, q):
        east_out[step, q] = product(mats[1, BACK_EAST], split_rows(field[step, q, 1]))
        west_copy[step][q].start()

    def push_south(step, q, i, d):
        south_out[step, q, d] = product(mats[d, BACK_SOUTH], split_rows(field[step, q, d]))
        north_copy[step][q][i].start()

    load_vec.wait()
    for q in chunks:
        field[0, q, mine] = vec_ref[:, columns(mine, q)]
    load_blocks.wait()
    assemble_side(blocks_ref, code, mine, 1, FWD_EAST, BACK_EAST)

    @odd
    def _():
        for q in chunks:
            push_east(0, q)

    assemble_side(blocks_ref, code, mine, 2, FWD_SOUTH, BACK_SOUTH)
    for q in chunks:
        push_south(0, q, 0, mine)
    assemble_own(blocks_ref, code, mine)

    got_field[0].wait_recv()
    odd(east_copy[0][0].start)
    south_copy[0][0][1].start()

    got_code.wait_recv()
    got_blocks.wait_recv()
    assemble_side(blocks_in, code_in, other, 1, FWD_EAST, BACK_EAST)

    @even
    def _():
        push_east(0, 0)

    assemble_side(blocks_in, code_in, other, 2, FWD_SOUTH, BACK_SOUTH)
    push_south(0, 0, 1, other)
    for q in chunks[1:]:
        got_field[q].wait_recv()
        odd(east_copy[0][q].start)
        south_copy[0][q][1].start()

        @even
        def _():
            push_east(0, q)

        push_south(0, q, 1, other)
    assemble_own(blocks_in, code_in, other)

    def inside(step, q):
        first, second = split_rows(field[step, q, 0]), split_rows(field[step, q, 1])
        acc[q, 0] = product(mats[0, SYM], first) + product(mats[0, FWD_EAST], second)
        acc[q, 1] = product(mats[0, BACK_EAST], first) + product(mats[1, SYM], second)

    for q in chunks:
        inside(0, q)

    centre = spectrum_ref[0]
    inverse = 1.0 / spectrum_ref[1]

    def wait_row(step, q, i):
        south_copy[step][q][i].wait_recv()
        north_copy[step][q][i].wait_recv()

    def upper(step, q):
        total = acc[q, 0] + product(mats[0, FWD_SOUTH], split_rows(south[step, q, 0]))
        total = total + north_in[step, q, 0]
        west_copy[step][q].wait_recv()
        return (total + west_in[step, q] - centre * field[step, q, 0]) * inverse

    def lower(step, q):
        total = acc[q, 1] + product(mats[1, FWD_SOUTH], split_rows(south[step, q, 1]))
        total = total + north_in[step, q, 1]
        east_copy[step][q].wait_recv()
        total = total + product(mats[1, FWD_EAST], split_rows(east[step, q]))
        return (total - centre * field[step, q, 1]) * inverse

    for q in chunks:
        wait_row(0, q, 0)
        wait_row(0, q, 1)
        field[1, q, 0] = upper(0, q)
        even(east_copy[1][q].start)
        field[1, q, 1] = lower(0, q)
        south_copy[1][q][1].start()
        push_east(1, q)
        odd(east_copy[1][q].start)
        push_south(1, q, 1, other)
        south_copy[1][q][0].start()
        push_south(1, q, 0, mine)
    for q in chunks:
        inside(1, q)

    keep = []
    last = [remote(field.at[2, q, other], out_ref.at[:, columns(mine, q)], to_partner) for q in chunks]

    def set_upper(q):
        field[2, q, 0] = 2.0 * upper(1, q) - field[0, q, 0]

    def set_lower(q):
        field[2, q, 1] = 2.0 * lower(1, q) - field[0, q, 1]

    for q in chunks:
        wait_row(1, q, 1)
        even(functools.partial(set_lower, q))
        odd(functools.partial(set_upper, q))
        last[q].start()
        wait_row(1, q, 0)
        even(functools.partial(set_upper, q))
        odd(functools.partial(set_lower, q))
        keep.append(pltpu.make_async_copy(field.at[2, q, mine], out_ref.at[:, columns(mine, q)], load_sem.at[2 + q]))
        keep[q].start()

    for copy in keep:
        copy.wait()
    for copy in last:
        copy.wait_recv()
    for copy in made:
        copy.wait_send()


def local(row_count, col_count, vectors, blocks, place, live, spectrum):
    rows, width = vectors.shape
    slots, bs, _ = blocks.shape
    wide = width // 2 // CHUNKS
    f32 = jnp.float32
    copies = 2 + CHUNKS * (1 + 4 + 4 + 2 + 2 + 1)
    vmem = pl.BlockSpec(memory_space=pltpu.VMEM)
    hbm = pl.BlockSpec(memory_space=pltpu.HBM)
    smem = pl.BlockSpec(memory_space=pltpu.SMEM)
    return pl.pallas_call(
        functools.partial(kernel, row_count, col_count),
        out_shape=jax.ShapeDtypeStruct((rows, width), f32),
        in_specs=[hbm, hbm, smem, smem, smem],
        out_specs=hbm,
        scratch_shapes=[
            pltpu.VMEM((rows, width), f32),
            pltpu.VMEM((slots, bs, bs), f32),
            pltpu.VMEM((8, bs), f32),
            pltpu.VMEM((8, bs), f32),
            pltpu.VMEM((slots, bs, bs), f32),
            pltpu.VMEM((2, 5, rows, 3 * rows), jnp.bfloat16),
            pltpu.VMEM((3, CHUNKS, 2, rows, wide), f32),
            pltpu.VMEM((2, CHUNKS, 2, rows, wide), f32),
            pltpu.VMEM((2, CHUNKS, 2, rows, wide), f32),
            pltpu.VMEM((2, CHUNKS, 2, rows, wide), f32),
            pltpu.VMEM((2, CHUNKS, rows, wide), f32),
            pltpu.VMEM((2, CHUNKS, rows, wide), f32),
            pltpu.VMEM((2, CHUNKS, rows, wide), f32),
            pltpu.VMEM((CHUNKS, 2, rows, wide), f32),
            pltpu.SemaphoreType.DMA((2 + CHUNKS,)),
            pltpu.SemaphoreType.DMA((copies,)),
            pltpu.SemaphoreType.DMA((copies,)),
        ],
        compiler_params=pltpu.CompilerParams(
            collective_id=0, has_side_effects=True, vmem_limit_bytes=60 * 1024 * 1024
        ),
        name="chebyshev_pair",
    )(vectors, blocks, place.T, live, spectrum)


def solution(mesh):
    return jax.shard_map(
        functools.partial(local, mesh.shape["row"], mesh.shape["col"]),
        mesh=mesh,
        in_specs=(
            P(("row", "col"), None),
            P(("row", "col"), None, None),
            P(("row", "col"), None),
            P(("row", "col")),
            P(),
        ),
        out_specs=P(("row", "col"), None),
        check_vma=False,
    )
```

```python
import functools

import jax
import jax.numpy as jnp
from jax import lax
from jax.experimental import pallas as pl
from jax.experimental.pallas import tpu as pltpu
from jax.sharding import PartitionSpec as P


CHUNKS = 2
SYM, FWD_EAST, BACK_EAST, FWD_SOUTH, BACK_SOUTH = range(5)
MESH = pl.DeviceIdType.MESH


def split_rows(x):
    high = x.astype(jnp.bfloat16)
    low = (x - high.astype(jnp.float32)).astype(jnp.bfloat16)
    return jnp.concatenate([high, high, low], axis=0)


def split_columns(x):
    high = x.astype(jnp.bfloat16)
    low = (x - high.astype(jnp.float32)).astype(jnp.bfloat16)
    return jnp.concatenate([high, low, high], axis=1)


def product(matrix, x):
    return jnp.dot(matrix, x, preferred_element_type=jnp.float32)


def kernel(
    row_count,
    col_count,
    vec_hbm,
    blocks_hbm,
    place_ref,
    live_ref,
    spectrum_ref,
    out_ref,
    vec_ref,
    blocks_ref,
    code,
    code_in,
    blocks_in,
    mats,
    field,
    south,
    south_out,
    north_in,
    east,
    east_out,
    west_in,
    acc,
    load_sem,
    send_sem,
    recv_sem,
):
    rows, width = vec_ref.shape
    slots, bs, _ = blocks_ref.shape
    panels = rows // bs
    half = width // 2
    wide = half // CHUNKS

    load_blocks = pltpu.make_async_copy(blocks_hbm, blocks_ref, load_sem.at[0])
    load_blocks.start()
    load_vec = pltpu.make_async_copy(vec_hbm, vec_ref, load_sem.at[1])
    load_vec.start()

    me_row, me_col = lax.axis_index("row"), lax.axis_index("col")
    mine = lax.rem(me_col, 2)
    other = 1 - mine
    to_partner = (me_row, me_col + 1 - 2 * mine)
    to_north = (lax.rem(me_row + row_count - 1, row_count), me_col)
    to_south = (lax.rem(me_row + 1, row_count), me_col)
    to_west = (me_row, lax.rem(me_col + col_count - 2, col_count))
    to_east = (me_row, lax.rem(me_col + 2, col_count))

    barrier = pltpu.get_barrier_semaphore()
    for device in (to_partner, to_north, to_south, to_west, to_east):
        pl.semaphore_signal(barrier, inc=1, device_id=device, device_id_type=MESH)

    live = live_ref[0]
    for s in range(slots):
        value = (place_ref[0, s] * 3 + place_ref[1, s]) * panels + place_ref[2, s]
        value = jnp.where(s < live, value, -1)
        code[s : s + 1, :] = jnp.full((1, bs), value, jnp.int32).astype(jnp.float32)
    pl.semaphore_wait(barrier, 5)

    made = []

    def remote(src, dst, device, reuse=None):
        index = len(made) if reuse is None else reuse
        copy = pltpu.make_async_remote_copy(
            src_ref=src,
            dst_ref=dst,
            send_sem=send_sem.at[index],
            recv_sem=recv_sem.at[index],
            device_id=device,
            device_id_type=MESH,
        )
        if reuse is None:
            made.append(copy)
        return copy

    def send(src, dst, device):
        copy = remote(src, dst, device)
        copy.start()
        return copy

    def columns(which, q):
        return pl.ds(pl.multiple_of(which * half + q * wide, wide), wide)

    def even(body):
        pl.when(mine == 0)(body)

    def odd(body):
        pl.when(mine == 1)(body)

    chunks = range(CHUNKS)
    both = range(2)

    got_code = send(code, code_in, to_partner)
    got_field = [send(vec_hbm.at[:, columns(other, 0)], field.at[0, 0, mine], to_partner)]
    got_blocks = send(blocks_hbm, blocks_in, to_partner)
    for q in chunks[1:]:
        got_field.append(send(vec_hbm.at[:, columns(other, q)], field.at[0, q, mine], to_partner))

    south_copy = [[[None] * 2 for _ in chunks] for _ in both]
    north_copy = [[[None] * 2 for _ in chunks] for _ in both]
    for step in both:
        for q in chunks:
            for i, d in enumerate((mine, other)):
                src = field.at[step, q, d]
                if step == 0 and i == 0:
                    src = vec_hbm.at[:, columns(mine, q)]
                south_copy[step][q][i] = remote(src, south.at[step, q, d], to_north)
                north_copy[step][q][i] = remote(south_out.at[step, q, d], north_in.at[step, q, d], to_south)
    east_index = len(made)
    east_copy = [[remote(field.at[step, q, 0], east.at[step, q], to_west) for q in chunks] for step in both]
    west_copy = [[remote(east_out.at[step, q], west_in.at[step, q], to_east) for q in chunks] for step in both]
    early = [
        remote(vec_hbm.at[:, columns(mine, q)], east.at[0, q], to_west, east_index + q) for q in chunks
    ]

    for q in chunks:
        even(early[q].start)
        south_copy[0][q][0].start()

    def dense(source, codes, t):
        columns_of = []
        for b in range(panels):
            parts = []
            for a in range(panels):
                total = None
                for s in range(slots):
                    weight = jnp.where(codes[s : s + 1, :] == float((a * 3 + t) * panels + b), 1.0, 0.0)
                    term = source[s] * weight
                    total = term if total is None else total + term
                parts.append(total)
            columns_of.append(jnp.concatenate(parts, axis=0))
        return jnp.concatenate(columns_of, axis=1)

    def assemble_side(source, codes, domain, t, forward, back):
        matrix = dense(source, codes, t)
        mats[domain, back] = split_columns(matrix.T)
        mats[domain, forward] = split_columns(matrix)

    def assemble_own(source, codes, domain):
        matrix = dense(source, codes, 0)
        mats[domain, SYM] = split_columns(matrix + matrix.T)

    def push_east(step, q):
        east_out[step, q] = product(mats[1, BACK_EAST], split_rows(field[step, q, 1]))
        west_copy[step][q].start()

    def push_south(step, q, i, d):
        south_out[step, q, d] = product(mats[d, BACK_SOUTH], split_rows(field[step, q, d]))
        north_copy[step][q][i].start()

    load_vec.wait()
    for q in chunks:
        field[0, q, mine] = vec_ref[:, columns(mine, q)]
    load_blocks.wait()
    assemble_side(blocks_ref, code, mine, 1, FWD_EAST, BACK_EAST)

    @odd
    def _():
        for q in chunks:
            push_east(0, q)

    assemble_side(blocks_ref, code, mine, 2, FWD_SOUTH, BACK_SOUTH)
    for q in chunks:
        push_south(0, q, 0, mine)
    assemble_own(blocks_ref, code, mine)

    got_field[0].wait_recv()
    odd(east_copy[0][0].start)
    south_copy[0][0][1].start()

    got_code.wait_recv()
    got_blocks.wait_recv()
    assemble_side(blocks_in, code_in, other, 1, FWD_EAST, BACK_EAST)

    @even
    def _():
        push_east(0, 0)

    assemble_side(blocks_in, code_in, other, 2, FWD_SOUTH, BACK_SOUTH)
    push_south(0, 0, 1, other)
    for q in chunks[1:]:
        got_field[q].wait_recv()
        odd(east_copy[0][q].start)
        south_copy[0][q][1].start()

        @even
        def _():
            push_east(0, q)

        push_south(0, q, 1, other)
    assemble_own(blocks_in, code_in, other)

    def inside(step, q):
        first, second = split_rows(field[step, q, 0]), split_rows(field[step, q, 1])
        acc[q, 0] = product(mats[0, SYM], first) + product(mats[0, FWD_EAST], second)
        acc[q, 1] = product(mats[0, BACK_EAST], first) + product(mats[1, SYM], second)

    for q in chunks:
        inside(0, q)

    centre = spectrum_ref[0]
    inverse = 1.0 / spectrum_ref[1]

    def wait_row(step, q, i):
        south_copy[step][q][i].wait_recv()
        north_copy[step][q][i].wait_recv()

    def upper(step, q):
        total = acc[q, 0] + product(mats[0, FWD_SOUTH], split_rows(south[step, q, 0]))
        total = total + north_in[step, q, 0]
        west_copy[step][q].wait_recv()
        return (total + west_in[step, q] - centre * field[step, q, 0]) * inverse

    def lower(step, q):
        total = acc[q, 1] + product(mats[1, FWD_SOUTH], split_rows(south[step, q, 1]))
        total = total + north_in[step, q, 1]
        east_copy[step][q].wait_recv()
        total = total + product(mats[1, FWD_EAST], split_rows(east[step, q]))
        return (total - centre * field[step, q, 1]) * inverse

    for q in chunks:
        wait_row(0, q, 0)
        wait_row(0, q, 1)
        field[1, q, 0] = upper(0, q)
        even(east_copy[1][q].start)
        field[1, q, 1] = lower(0, q)
        south_copy[1][q][1].start()
        push_east(1, q)
        odd(east_copy[1][q].start)
        push_south(1, q, 1, other)
        south_copy[1][q][0].start()
        push_south(1, q, 0, mine)
    for q in chunks:
        inside(1, q)

    keep = []
    last = [remote(field.at[2, q, other], out_ref.at[:, columns(mine, q)], to_partner) for q in chunks]

    def set_upper(q):
        field[2, q, 0] = 2.0 * upper(1, q) - field[0, q, 0]

    def set_lower(q):
        field[2, q, 1] = 2.0 * lower(1, q) - field[0, q, 1]

    for q in chunks:
        wait_row(1, q, 1)
        even(functools.partial(set_lower, q))
        odd(functools.partial(set_upper, q))
        last[q].start()
        wait_row(1, q, 0)
        even(functools.partial(set_upper, q))
        odd(functools.partial(set_lower, q))
        keep.append(pltpu.make_async_copy(field.at[2, q, mine], out_ref.at[:, columns(mine, q)], load_sem.at[2 + q]))
        keep[q].start()

    for copy in keep:
        copy.wait()
    for copy in last:
        copy.wait_recv()
    for copy in made:
        copy.wait_send()


def local(row_count, col_count, vectors, blocks, place, live, spectrum):
    rows, width = vectors.shape
    slots, bs, _ = blocks.shape
    wide = width // 2 // CHUNKS
    f32 = jnp.float32
    copies = 2 + CHUNKS * (1 + 4 + 4 + 2 + 2 + 1)
    vmem = pl.BlockSpec(memory_space=pltpu.VMEM)
    hbm = pl.BlockSpec(memory_space=pltpu.HBM)
    smem = pl.BlockSpec(memory_space=pltpu.SMEM)
    return pl.pallas_call(
        functools.partial(kernel, row_count, col_count),
        out_shape=jax.ShapeDtypeStruct((rows, width), f32),
        in_specs=[hbm, hbm, smem, smem, smem],
        out_specs=hbm,
        scratch_shapes=[
            pltpu.VMEM((rows, width), f32),
            pltpu.VMEM((slots, bs, bs), f32),
            pltpu.VMEM((8, bs), f32),
            pltpu.VMEM((8, bs), f32),
            pltpu.VMEM((slots, bs, bs), f32),
            pltpu.VMEM((2, 5, rows, 3 * rows), jnp.bfloat16),
            pltpu.VMEM((3, CHUNKS, 2, rows, wide), f32),
            pltpu.VMEM((2, CHUNKS, 2, rows, wide), f32),
            pltpu.VMEM((2, CHUNKS, 2, rows, wide), f32),
            pltpu.VMEM((2, CHUNKS, 2, rows, wide), f32),
            pltpu.VMEM((2, CHUNKS, rows, wide), f32),
            pltpu.VMEM((2, CHUNKS, rows, wide), f32),
            pltpu.VMEM((2, CHUNKS, rows, wide), f32),
            pltpu.VMEM((CHUNKS, 2, rows, wide), f32),
            pltpu.SemaphoreType.DMA((2 + CHUNKS,)),
            pltpu.SemaphoreType.DMA((copies,)),
            pltpu.SemaphoreType.DMA((copies,)),
        ],
        compiler_params=pltpu.CompilerParams(
            collective_id=0, has_side_effects=True, vmem_limit_bytes=60 * 1024 * 1024
        ),
        name="chebyshev_pair",
    )(vectors, blocks, place.T, live, spectrum)


def solution(mesh):
    return jax.shard_map(
        functools.partial(local, mesh.shape["row"], mesh.shape["col"]),
        mesh=mesh,
        in_specs=(
            P(("row", "col"), None),
            P(("row", "col"), None, None),
            P(("row", "col"), None),
            P(("row", "col")),
            P(),
        ),
        out_specs=P(("row", "col"), None),
        check_vma=False,
    )
```
